32 devices in a mesh: row: 8 (over z, x), col: 4 (over y, core).
Axes of the slice: x: 2, y: 2, z: 4, core: 2. Of those that a mesh axis runs over, the one named last changes fastest.
Arguments:
- query_grads: bfloat16 [27648, 256], P(('row', 'col')), may hold values from -6 to 6
- eigenbasis: bfloat16 [27648, 27648], P('row', 'col'), may hold values from -0.0546875 to 0.0546875
- eigenvalues: float32 [27648], P('col'), may hold values from 0.05 to 20
- activations: bfloat16 [1024, 8, 3456], P('row', None, 'col'), may hold values from -0.0390625 to 0.0390625
Outputs:
- scores: float32 [256, 1024], P('col', 'row')
The draws below stay inside these ranges and needn't reach their ends.
All inputs are finite; a program needn't handle non-finite values.
Results may differ from the reference program's by a relative error of at most 0.0037.
Values may be sent and summed in bfloat16 or wider, within the bound.
A program may use at most 128 MiB of HBM per device.

```python
import math
import jax
import jax.numpy as jnp
from jax import lax

N = 27648
QUERIES = 256
TOKENS = 1024
N_ROW = 8


def with_spikes(drawn, rng, source, target, blocks, factor):
    owner, partner = [(jnp.arange(drawn.shape[dim]) // (drawn.shape[dim] // blocks)).reshape([-1 if axis == dim else 1 for axis in range(drawn.ndim)]) for dim in (source, target)]
    chosen = jax.random.permutation(rng, blocks)[partner]
    strong = (owner == chosen) | (owner == (partner + blocks // 2) % blocks)
    return jnp.where(strong, factor * drawn, drawn)


def shard_levels(rng, shape, pieces, least, high):
    factor_of, own = 1.0, jax.random.fold_in(rng, 6)
    for position, parts in pieces:
        steps = jnp.exp(jax.random.uniform(jax.random.fold_in(own, position), (parts,), jnp.float32, least / len(pieces), high / len(pieces)))
        factor_of = factor_of * jnp.repeat(steps, shape[position] // parts).reshape([-1 if axis == position else 1 for axis in range(len(shape))])
    return factor_of


def normal_values(key, extent, spread, reach, shards=(), held_as=jnp.bfloat16):
    gain = shard_levels(key, extent, shards, -0.22, 0.18) if shards else 1.0
    entries = jax.random.normal(key, extent, jnp.float32) * spread * gain
    return jnp.minimum(jnp.maximum(entries, -reach), reach).astype(held_as)


def bell_draw_with(own_key, extent, deviation, limit, split, heavy, held_as=jnp.bfloat16):
    drawn = deviation * jax.random.normal(own_key, extent, jnp.float32)
    if split:
        drawn = drawn * shard_levels(own_key, extent, split, -0.22, 0.18)
    return jnp.clip(with_spikes(drawn, jax.random.fold_in(own_key, 3), *heavy), -limit, limit).astype(held_as)


def setup_inputs(seed: int = 0) -> dict:
    splits = jax.random.split(jax.random.key(seed), 5)
    query_grads = normal_values(splits[0], (N, QUERIES), 1.0, 6.0, ((0, 32),))
    eigenbasis = bell_draw_with(splits[1], (N, N), N ** -0.5, 0.0546875, ((0, 8), (1, 4)), (0, 1, 8, 2.0))
    eigenvalues = jnp.clip(jnp.exp(math.log(20.0) - 5.9914645 * jax.random.uniform(splits[2], (N,), jnp.float32) ** shard_levels(splits[2], (N,), ((0, 4),), -0.2, 0.2)), 0.05, 20.0)
    activations = normal_values(splits[3], (TOKENS, N_ROW, N // N_ROW), N ** -0.5, 0.0390625, ((0, 8), (2, 4)))
    return {"query_grads": query_grads, "eigenbasis": eigenbasis, "eigenvalues": eigenvalues, "activations": activations}


def reference(query_grads, eigenbasis, eigenvalues, activations):
    rotated = lax.dot_general(eigenbasis, query_grads, (((0,), (0,)), ((), ())), preferred_element_type=jnp.float32)
    factor = (1.0 - jnp.exp(-eigenvalues)) / eigenvalues
    filtered = (rotated * factor[:, None]).astype(jnp.bfloat16)
    restored = jnp.dot(eigenbasis, filtered, preferred_element_type=jnp.float32).astype(jnp.bfloat16)
    flat = activations.reshape(activations.shape[0], -1)
    return lax.dot_general(restored, flat, (((0,), (1,)), ((), ())), preferred_element_type=jnp.float32)
```

```python
import functools

import jax
import jax.numpy as jnp
from jax import lax
from jax.experimental import pallas as pl
from jax.experimental.pallas import tpu as pltpu
from jax.sharding import PartitionSpec as P

CHUNKS = 9
LAG = 6
F32, BF16 = jnp.float32, jnp.bfloat16
NT = (((1,), (1,)), ((), ()))


def filter_weights(values):
    return (1.0 - jnp.exp(-values)) / values


def kernel(
    gt_ref, u_ref, w_ref, act_ref, out_ref,
    gt, u1, u2, part, send, recv, filt, rest, core_in, y_out, y_in,
    acts, tot, tot_core, tot_y, tot_row,
    u1_sem, u2_sem, g_send, g_recv, a_send, a_recv, a_own, x_send, x_recv,
    r_send, r_recv, t_send, t_recv,
):
    row, col = lax.axis_index("row"), lax.axis_index("col")
    b0, b1, b2 = lax.rem(row, 2), lax.rem(lax.div(row, 2), 2), lax.div(row, 4)
    core, y = lax.rem(col, 2), lax.div(col, 2)
    peers = (row + 1 - 2 * b0, row + 2 - 4 * b1, row + 4 - 8 * b2)
    core_peer, y_peer = col + 1 - 2 * core, col + 2 - 4 * y
    mc = u1.shape[2]
    depth = gt.shape[2]

    def copy(src, dst, ssem, rsem, r, c):
        return pltpu.make_async_remote_copy(
            src_ref=src, dst_ref=dst, send_sem=ssem, recv_sem=rsem,
            device_id=(r, c), device_id_type=pl.DeviceIdType.MESH,
        )

    def load(c, buf, sem):
        slot = lax.rem(c, 2)
        cols = pl.ds(pl.multiple_of(c * mc, 128), mc)
        return pltpu.make_async_copy(u_ref.at[:, cols], buf.at[slot], sem.at[slot])

    load(0, u1, u1_sem).start()

    barrier = pltpu.get_barrier_semaphore()
    for d in range(1, 8):
        pl.semaphore_signal(barrier, inc=1, device_id=(lax.rem(row + d, 8), col),
                            device_id_type=pl.DeviceIdType.MESH)
    for c in (core_peer, y_peer):
        pl.semaphore_signal(barrier, inc=1, device_id=(row, c),
                            device_id_type=pl.DeviceIdType.MESH)
    pl.semaphore_wait(barrier, 9)

    own_y = copy(gt_ref, gt.at[col], g_send.at[0], g_recv.at[0], row, y_peer)
    own_c = copy(gt_ref, gt.at[col], g_send.at[1], g_recv.at[1], row, core_peer)
    own_y.start()
    own_c.start()
    gt[col] = gt_ref[...]

    own_a = pltpu.make_async_copy(act_ref.at[row], acts.at[row], a_own)
    own_a.start()

    def act_copy(d):
        to = lax.rem(row + d, 8)
        return copy(act_ref.at[to], acts.at[row], a_send.at[d], a_recv.at[d], to, col)

    def act_arrival(d):
        origin = lax.rem(row + 8 - d, 8)
        return copy(act_ref.at[row], acts.at[origin], a_send.at[d], a_recv.at[d], origin, col)

    for d in range(1, 8):
        act_copy(d).start()

    rest[...] = jnp.zeros_like(rest)

    copy(gt_ref, gt.at[y_peer], g_send.at[0], g_recv.at[0], row, y_peer).wait_recv()
    fwd = copy(gt.at[y_peer], gt.at[y_peer], g_send.at[2], g_recv.at[2], row, core_peer)
    fwd.start()
    copy(gt_ref, gt.at[core_peer], g_send.at[1], g_recv.at[1], row, core_peer).wait_recv()
    diagonal = (1 - y) * 2 + 1 - core
    copy(gt.at[y_peer], gt.at[diagonal], g_send.at[2], g_recv.at[2], row, core_peer).wait_recv()

    def rows(start, size):
        return pl.ds(pl.multiple_of(start, 32), size)

    keep = (rows(128 * b0, 128), rows(128 * b0 + 64 * b1, 64), rows(128 * b0 + 64 * b1 + 32 * b2, 32))
    give = (
        rows(128 * (1 - b0), 128),
        rows(128 * b0 + 64 * (1 - b1), 64),
        rows(128 * b0 + 64 * b1 + 32 * (1 - b2), 32),
    )
    slab = (pl.ds(0, 128), pl.ds(128, 64), pl.ds(192, 32))

    def halving(c, k):
        return copy(send.at[c, slab[k]], recv.at[c, slab[k]], x_send.at[k, c], x_recv.at[k, c],
                    peers[k], col)

    def doubling(c, k):
        return copy(filt.at[c, keep[k]], filt.at[c, keep[k]], x_send.at[3 + k, c],
                    x_recv.at[3 + k, c], peers[k], col)

    def doubled(c, k):
        return copy(filt.at[c, give[k]], filt.at[c, give[k]], x_send.at[3 + k, c],
                    x_recv.at[3 + k, c], peers[k], col)

    def hand_on(c, k):
        send[c, slab[k]] = part[c, give[k]].astype(BF16)
        halving(c, k).start()

    def stage(s, lag, body):
        c = s - lag
        pl.when(jnp.logical_and(c >= 0, c < CHUNKS))(lambda: body(c))

    def gathered(c):
        doubled(c, 1).wait_recv()
        doubling(c, 0).start()

    def gather(c):
        doubled(c, 2).wait_recv()
        doubling(c, 1).start()

    def scale(c):
        halving(c, 2).wait_recv()
        total = part[c, keep[2]] + recv[c, slab[2]].astype(F32)
        filt[c, keep[2]] = (total * w_ref[c]).astype(BF16)
        doubling(c, 2).start()

    def add(k):
        def body(c):
            halving(c, k).wait_recv()
            part[c, keep[k]] += recv[c, slab[k]].astype(F32)
            hand_on(c, k + 1)
        return body

    def rotate(c):
        slot = lax.rem(c, 2)
        load(c, u1, u1_sem).wait()
        pl.when(c + 1 < CHUNKS)(lambda: load(c + 1, u1, u1_sem).start())

        def tile(t, carry):
            cols = pl.ds(pl.multiple_of(t * 256, 256), 256)
            total = jnp.zeros((256, 256), F32)
            for j in range(4):
                total += jnp.dot(gt[j], u1[slot, pl.ds(j * depth, depth), cols],
                                 preferred_element_type=F32)
            part[c, :, cols] = total
            return carry

        lax.fori_loop(0, mc // 256, tile, 0)
        hand_on(c, 0)

    def restore(c):
        slot = lax.rem(c, 2)
        load(c, u2, u2_sem).wait()
        doubled(c, 0).wait_recv()

        def block(j, carry):
            n = pl.ds(pl.multiple_of(j * depth, 16), depth)
            rest[j] += lax.dot_general(filt[c], u2[slot, n, :], NT, preferred_element_type=F32)
            return carry

        lax.fori_loop(0, 4, block, 0)

    def step(s, carry):
        stage(s, 5, gathered)
        stage(s, 4, gather)
        stage(s, 3, scale)
        stage(s, 2, add(1))
        stage(s, 1, add(0))
        stage(s, 0, rotate)
        stage(s, LAG - 1, lambda c: load(c, u2, u2_sem).start())
        stage(s, LAG, restore)
        return carry

    lax.fori_loop(0, CHUNKS + LAG, step, 0)

    def across(k):
        return copy(rest.at[2 * k + 1 - core], core_in.at[k], r_send.at[k], r_recv.at[k],
                    row, core_peer)

    for k in range(2):
        across(k).start()

    def reach_y():
        return copy(y_out, y_in, r_send.at[2], r_recv.at[2], row, y_peer)

    for k in range(2):
        across(k).wait_recv()
    y_out[...] = (rest[2 * (1 - y) + core] + core_in[1 - y]).astype(BF16)
    reach_y().start()
    for d in range(1, 8):
        act_arrival(d).wait_recv()
    own_a.wait()
    kept = rest[col] + core_in[y]
    reach_y().wait_recv()
    restored = (kept + y_in[...].astype(F32)).astype(BF16)
    for t in range(8):
        place = (t % 2) * 4 + (t // 2 % 2) * 2 + t // 4
        scores = lax.dot_general(restored, acts[t], NT, preferred_element_type=F32)
        for q in range(4):
            tot[q, place] = scores[q * 64:(q + 1) * 64]

    def total_core(k):
        return copy(tot.at[2 * k + 1 - core], tot_core.at[k], t_send.at[k], t_recv.at[k],
                    row, core_peer)

    total_core(1 - y).start()
    total_core(y).start()
    total_core(1 - y).wait_recv()
    total_core(y).wait_recv()
    tot[2 * (1 - y) + core] += tot_core[1 - y]
    total_y = copy(tot.at[2 * (1 - y) + core], tot_y, t_send.at[2], t_recv.at[2], row, y_peer)
    total_y.start()
    tot[col] += tot_core[y]
    total_y.wait_recv()
    tot[col] += tot_y[...]

    at = 0
    row_sends = []
    for k, (size, bit) in enumerate(((4, b0), (2, b1), (1, b2))):
        mine, other = at + size * bit, at + size * (1 - bit)
        landing = tot_row.at[pl.ds((0, 4, 6)[k], size)]
        move = copy(tot.at[col, pl.ds(other, size)], landing, t_send.at[3 + k], t_recv.at[3 + k],
                    peers[k], col)
        move.start()
        row_sends.append(move)
        move.wait_recv()
        if size > 1:
            tot[col, pl.ds(mine, size)] += landing[...]
        else:
            out_ref[...] = tot[col, mine] + tot_row[6]
        at = mine

    own_y.wait_send()
    own_c.wait_send()
    fwd.wait_send()
    for d in range(1, 8):
        act_copy(d).wait_send()

    def drain(c, carry):
        for k in range(3):
            halving(c, k).wait_send()
            doubling(c, k).wait_send()
        return carry

    lax.fori_loop(0, CHUNKS, drain, 0)
    for k in range(2):
        across(k).wait_send()
        total_core(k).wait_send()
    reach_y().wait_send()
    total_y.wait_send()
    for move in row_sends:
        move.wait_send()


def fused(query_grads, eigenbasis, eigenvalues, activations):
    depth, queries = query_grads.shape
    n, m = eigenbasis.shape
    mc = m // CHUNKS
    tokens = activations.shape[0]
    weights = filter_weights(eigenvalues).reshape(CHUNKS, 1, mc)
    dma = pltpu.SemaphoreType.DMA
    vmem = pl.BlockSpec(memory_space=pltpu.VMEM)
    hbm = pl.BlockSpec(memory_space=pl.ANY)
    return pl.pallas_call(
        kernel,
        out_shape=jax.ShapeDtypeStruct((queries // 4, tokens), F32),
        in_specs=[vmem, hbm, vmem, hbm],
        out_specs=vmem,
        scratch_shapes=[
            pltpu.VMEM((4, queries, depth), BF16),
            pltpu.VMEM((2, n, mc), BF16),
            pltpu.VMEM((2, n, mc), BF16),
            pltpu.VMEM((CHUNKS, queries, mc), F32),
            pltpu.VMEM((CHUNKS, 224, mc), BF16),
            pltpu.VMEM((CHUNKS, 224, mc), BF16),
            pltpu.VMEM((CHUNKS, queries, mc), BF16),
            pltpu.VMEM((4, queries, depth), F32),
            pltpu.VMEM((2, queries, depth), F32),
            pltpu.VMEM((queries, depth), BF16),
            pltpu.VMEM((queries, depth), BF16),
            pltpu.VMEM((8, tokens, depth), BF16),
            pltpu.VMEM((4, 8, queries // 4, tokens), F32),
            pltpu.VMEM((2, 8, queries // 4, tokens), F32),
            pltpu.VMEM((8, queries // 4, tokens), F32),
            pltpu.VMEM((7, queries // 4, tokens), F32),
            dma((2,)), dma((2,)),
            dma((3,)), dma((3,)),
            dma((8,)), dma((8,)), dma,
            dma((6, CHUNKS)), dma((6, CHUNKS)),
            dma((3,)), dma((3,)),
            dma((6,)), dma((6,)),
        ],
        compiler_params=pltpu.CompilerParams(
            collective_id=0, has_side_effects=True, vmem_limit_bytes=60 * 2**20
        ),
        cost_estimate=pl.CostEstimate(
            flops=4 * n * m * queries, bytes_accessed=4 * n * m, transcendentals=0
        ),
    )(query_grads.T, eigenbasis, weights, activations.transpose(1, 0, 2))


def general(query_grads, eigenbasis, eigenvalues, activations):
    grad_block = lax.all_gather(query_grads, "col", axis=0, tiled=True)
    share = eigenbasis.shape[1] // lax.axis_size("row")
    partial_rot = lax.psum_scatter(
        lax.dot_general(
            eigenbasis, grad_block, (((0,), (0,)), ((), ())), preferred_element_type=jnp.float32
        ),
        "row",
        scatter_dimension=0,
        tiled=True,
    )
    local_vals = lax.dynamic_slice_in_dim(eigenvalues, lax.axis_index("row") * share, share, 0)
    filtered = (partial_rot * filter_weights(local_vals)[:, None]).astype(jnp.bfloat16)
    whole_cols = lax.all_gather(filtered, "row", axis=0, tiled=True)
    restored = lax.psum_scatter(
        jnp.dot(eigenbasis, whole_cols, preferred_element_type=jnp.float32),
        "col",
        scatter_dimension=0,
        tiled=True,
    ).astype(jnp.bfloat16)
    blocks = lax.all_gather(restored, "row", axis=0, tiled=True)
    flat = activations.reshape(activations.shape[0], -1)
    return lax.psum_scatter(
        lax.dot_general(blocks, flat, (((0,), (1,)), ((), ())), preferred_element_type=jnp.float32),
        "col",
        scatter_dimension=0,
        tiled=True,
    )


def local(query_grads, eigenbasis, eigenvalues, activations):
    sizes = (lax.axis_size("row"), lax.axis_size("col"))
    fits = (
        sizes == (8, 4)
        and query_grads.shape[1] == 256
        and eigenbasis.shape[1] % (256 * CHUNKS) == 0
        and eigenbasis.shape[0] % 64 == 0
        and activations.shape[0] == 128
    )
    return (fused if fits else general)(query_grads, eigenbasis, eigenvalues, activations)


def solution(mesh):
    in_specs = (P(("row", "col"), None), P("row", "col"), P("col"), P("row", None, "col"))
    out_specs = P("col", "row")
    return jax.shard_map(local, mesh=mesh, in_specs=in_specs, out_specs=out_specs, check_vma=False)
```

```python
import functools

import jax
import jax.numpy as jnp
from jax import lax
from jax.experimental import pallas as pl
from jax.experimental.pallas import tpu as pltpu
from jax.sharding import PartitionSpec as P

CHUNKS = 9
LAG = 6
SPREAD = 4
F32, BF16 = jnp.float32, jnp.bfloat16
NT = (((1,), (1,)), ((), ()))


def filter_weights(values):
    return (1.0 - jnp.exp(-values)) / values


def kernel(
    gt_ref, u_ref, w_ref, act_ref, out_ref,
    gt, u1, u2, part, send, recv, filt, rest, core_in, y_out, y_in,
    acts, tot, tot_row,
    u1_sem, u2_sem, g_send, g_recv, a_send, a_recv, a_own, x_send, x_recv,
    r_send, r_recv, t_send, t_recv, s_send, s_recv,
):
    row, col = lax.axis_index("row"), lax.axis_index("col")
    b0, b1, b2 = lax.rem(row, 2), lax.rem(lax.div(row, 2), 2), lax.div(row, 4)
    core, y = lax.rem(col, 2), lax.div(col, 2)
    peers = (row + 1 - 2 * b0, row + 2 - 4 * b1, row + 4 - 8 * b2)
    core_peer, y_peer = col + 1 - 2 * core, col + 2 - 4 * y
    mc = u1.shape[2]
    depth = gt.shape[2]

    def copy(src, dst, ssem, rsem, r, c):
        return pltpu.make_async_remote_copy(
            src_ref=src, dst_ref=dst, send_sem=ssem, recv_sem=rsem,
            device_id=(r, c), device_id_type=pl.DeviceIdType.MESH,
        )

    def load(c, buf, sem):
        slot = lax.rem(c, 2)
        cols = pl.ds(pl.multiple_of(c * mc, 128), mc)
        return pltpu.make_async_copy(u_ref.at[:, cols], buf.at[slot], sem.at[slot])

    load(0, u1, u1_sem).start()

    barrier = pltpu.get_barrier_semaphore()
    for d in range(1, 8):
        pl.semaphore_signal(barrier, inc=1, device_id=(lax.rem(row + d, 8), col),
                            device_id_type=pl.DeviceIdType.MESH)
    for c in (core_peer, y_peer):
        pl.semaphore_signal(barrier, inc=1, device_id=(row, c),
                            device_id_type=pl.DeviceIdType.MESH)
    pl.semaphore_wait(barrier, 9)

    own_y = copy(gt_ref, gt.at[col], g_send.at[0], g_recv.at[0], row, y_peer)
    own_c = copy(gt_ref, gt.at[col], g_send.at[1], g_recv.at[1], row, core_peer)
    own_y.start()
    own_c.start()
    gt[col] = gt_ref[...]

    own_a = pltpu.make_async_copy(act_ref.at[row], acts.at[col, row], a_own)
    own_a.start()

    def act_copy(d):
        to = lax.rem(row + d, 8)
        return copy(act_ref.at[to], acts.at[col, row], a_send.at[d], a_recv.at[d], to, col)

    def act_arrival(d):
        origin = lax.rem(row + 8 - d, 8)
        return copy(act_ref.at[row], acts.at[col, origin], a_send.at[d], a_recv.at[d], origin, col)

    def block_of(c, d):
        return acts.at[c, lax.rem(row + 8 - d, 8)]

    def over_y(c, d):
        return copy(block_of(c, d), block_of(c, d), s_send.at[0, d], s_recv.at[0, d], row, y_peer)

    def over_core(c, d, k):
        return copy(block_of(c, d), block_of(c, d), s_send.at[k, d], s_recv.at[k, d],
                    row, core_peer)

    def spread(d):
        pl.when(d == 0)(lambda: own_a.wait())
        pl.when(d > 0)(lambda: act_arrival(d).wait_recv())
        over_y(col, d).start()
        over_core(col, d, 1).start()

    def relay(d):
        over_y(y_peer, d).wait_recv()
        over_core(y_peer, d, 2).start()

    for d in range(1, 8):
        act_copy(d).start()

    rest[...] = jnp.zeros_like(rest)

    copy(gt_ref, gt.at[y_peer], g_send.at[0], g_recv.at[0], row, y_peer).wait_recv()
    fwd = copy(gt.at[y_peer], gt.at[y_peer], g_send.at[2], g_recv.at[2], row, core_peer)
    fwd.start()
    copy(gt_ref, gt.at[core_peer], g_send.at[1], g_recv.at[1], row, core_peer).wait_recv()
    diagonal = (1 - y) * 2 + 1 - core
    copy(gt.at[y_peer], gt.at[diagonal], g_send.at[2], g_recv.at[2], row, core_peer).wait_recv()

    def rows(start, size):
        return pl.ds(pl.multiple_of(start, 32), size)

    keep = (rows(128 * b0, 128), rows(128 * b0 + 64 * b1, 64), rows(128 * b0 + 64 * b1 + 32 * b2, 32))
    give = (
        rows(128 * (1 - b0), 128),
        rows(128 * b0 + 64 * (1 - b1), 64),
        rows(128 * b0 + 64 * b1 + 32 * (1 - b2), 32),
    )
    slab = (pl.ds(0, 128), pl.ds(128, 64), pl.ds(192, 32))

    def halving(c, k):
        return copy(send.at[c, slab[k]], recv.at[c, slab[k]], x_send.at[k, c], x_recv.at[k, c],
                    peers[k], col)

    def doubling(c, k):
        return copy(filt.at[c, keep[k]], filt.at[c, keep[k]], x_send.at[3 + k, c],
                    x_recv.at[3 + k, c], peers[k], col)

    def doubled(c, k):
        return copy(filt.at[c, give[k]], filt.at[c, give[k]], x_send.at[3 + k, c],
                    x_recv.at[3 + k, c], peers[k], col)

    def hand_on(c, k):
        send[c, slab[k]] = part[c, give[k]].astype(BF16)
        halving(c, k).start()

    def stage(s, lag, body):
        c = s - lag
        pl.when(jnp.logical_and(c >= 0, c < CHUNKS))(lambda: body(c))

    def gathered(c):
        doubled(c, 1).wait_recv()
        doubling(c, 0).start()

    def gather(c):
        doubled(c, 2).wait_recv()
        doubling(c, 1).start()

    def scale(c):
        halving(c, 2).wait_recv()
        total = part[c, keep[2]] + recv[c, slab[2]].astype(F32)
        filt[c, keep[2]] = (total * w_ref[c]).astype(BF16)
        doubling(c, 2).start()

    def add(k):
        def body(c):
            halving(c, k).wait_recv()
            part[c, keep[k]] += recv[c, slab[k]].astype(F32)
            hand_on(c, k + 1)
        return body

    def rotate(c):
        slot = lax.rem(c, 2)
        load(c, u1, u1_sem).wait()
        pl.when(c + 1 < CHUNKS)(lambda: load(c + 1, u1, u1_sem).start())

        def tile(t, carry):
            cols = pl.ds(pl.multiple_of(t * 256, 256), 256)
            total = jnp.zeros((256, 256), F32)
            for j in range(4):
                total += jnp.dot(gt[j], u1[slot, pl.ds(j * depth, depth), cols],
                                 preferred_element_type=F32)
            part[c, :, cols] = total
            return carry

        lax.fori_loop(0, mc // 256, tile, 0)
        hand_on(c, 0)

    def restore(c):
        slot = lax.rem(c, 2)
        load(c, u2, u2_sem).wait()
        doubled(c, 0).wait_recv()

        def block(j, carry):
            n = pl.ds(pl.multiple_of(j * depth, 16), depth)
            rest[j] += lax.dot_general(filt[c], u2[slot, n, :], NT, preferred_element_type=F32)
            return carry

        lax.fori_loop(0, 4, block, 0)

    def step(s, carry):
        stage(s, LAG - 1, lambda c: load(c, u2, u2_sem).start())
        stage(s, 0, rotate)
        stage(s, 5, gathered)
        stage(s, 4, gather)
        stage(s, 3, scale)
        stage(s, 2, add(1))
        stage(s, 1, add(0))
        pl.when(jnp.logical_and(s >= SPREAD, s < SPREAD + 8))(lambda: spread(s - SPREAD))
        pl.when(jnp.logical_and(s >= SPREAD + 2, s < SPREAD + 10))(lambda: relay(s - SPREAD - 2))
        stage(s, LAG, restore)
        return carry

    lax.fori_loop(0, CHUNKS + LAG, step, 0)

    queries = out_ref.shape[0]

    def part_of(j):
        return pl.ds(pl.multiple_of(j * queries, queries), queries)

    def across(k):
        return copy(rest.at[:, part_of(2 * k + 1 - core)], core_in.at[k], r_send.at[k],
                    r_recv.at[k], row, core_peer)

    across(1 - y).start()
    across(y).start()

    def reach_y():
        return copy(y_out, y_in, r_send.at[2], r_recv.at[2], row, y_peer)

    across(1 - y).wait_recv()
    y_out[...] = (rest[:, part_of(2 * (1 - y) + core)] + core_in[1 - y]).astype(BF16)
    reach_y().start()
    across(y).wait_recv()
    core_in[y] += rest[:, part_of(col)]
    for d in range(8):
        over_core(core_peer, d, 1).wait_recv()
        over_core(diagonal, d, 2).wait_recv()
    reach_y().wait_recv()
    restored = core_in[y] + y_in[...].astype(F32)
    high = restored.astype(BF16)
    low = (restored - high.astype(F32)).astype(BF16)
    both = jnp.concatenate([high, low], axis=1)
    for t in range(8):
        place = (t % 2) * 4 + (t // 2 % 2) * 2 + t // 4
        scores = jnp.zeros((2 * queries, acts.shape[2]), F32)
        for j in range(4):
            scores += lax.dot_general(both[j], acts[j, t], NT, preferred_element_type=F32)
        tot[place] = scores[:queries] + scores[queries:]

    at = 0
    row_sends = []
    for k, (size, bit) in enumerate(((4, b0), (2, b1), (1, b2))):
        mine, other = at + size * bit, at + size * (1 - bit)
        landing = tot_row.at[pl.ds((0, 4, 6)[k], size)]
        move = copy(tot.at[pl.ds(other, size)], landing, t_send.at[k], t_recv.at[k],
                    peers[k], col)
        move.start()
        row_sends.append(move)
        move.wait_recv()
        if size > 1:
            tot[pl.ds(mine, size)] += landing[...]
        else:
            out_ref[...] = tot[mine] + tot_row[6]
        at = mine

    own_y.wait_send()
    own_c.wait_send()
    fwd.wait_send()
    for d in range(1, 8):
        act_copy(d).wait_send()

    def drain(c, carry):
        for k in range(3):
            halving(c, k).wait_send()
            doubling(c, k).wait_send()
        return carry

    lax.fori_loop(0, CHUNKS, drain, 0)
    for k in range(2):
        across(k).wait_send()
    reach_y().wait_send()
    for d in range(8):
        over_y(col, d).wait_send()
        over_core(col, d, 1).wait_send()
        over_core(y_peer, d, 2).wait_send()
    for move in row_sends:
        move.wait_send()


def fused(query_grads, eigenbasis, eigenvalues, activations):
    depth, queries = query_grads.shape
    n, m = eigenbasis.shape
    mc = m // CHUNKS
    tokens = activations.shape[0]
    weights = filter_weights(eigenvalues).reshape(CHUNKS, 1, mc)
    dma = pltpu.SemaphoreType.DMA
    vmem = pl.BlockSpec(memory_space=pltpu.VMEM)
    hbm = pl.BlockSpec(memory_space=pl.ANY)
    return pl.pallas_call(
        kernel,
        out_shape=jax.ShapeDtypeStruct((queries // 4, tokens), F32),
        in_specs=[vmem, hbm, vmem, hbm],
        out_specs=vmem,
        scratch_shapes=[
            pltpu.VMEM((4, queries, depth), BF16),
            pltpu.VMEM((2, n, mc), BF16),
            pltpu.VMEM((2, n, mc), BF16),
            pltpu.VMEM((CHUNKS, queries, mc), F32),
            pltpu.VMEM((CHUNKS, 224, mc), BF16),
            pltpu.VMEM((CHUNKS, 224, mc), BF16),
            pltpu.VMEM((CHUNKS, queries, mc), BF16),
            pltpu.VMEM((4, queries, depth), F32),
            pltpu.VMEM((2, 4, queries // 4, depth), F32),
            pltpu.VMEM((4, queries // 4, depth), BF16),
            pltpu.VMEM((4, queries // 4, depth), BF16),
            pltpu.VMEM((4, 8, tokens, depth), BF16),
            pltpu.VMEM((8, queries // 4, tokens), F32),
            pltpu.VMEM((7, queries // 4, tokens), F32),
            dma((2,)), dma((2,)),
            dma((3,)), dma((3,)),
            dma((8,)), dma((8,)), dma,
            dma((6, CHUNKS)), dma((6, CHUNKS)),
            dma((3,)), dma((3,)),
            dma((3,)), dma((3,)),
            dma((3, 8)), dma((3, 8)),
        ],
        compiler_params=pltpu.CompilerParams(
            collective_id=0, has_side_effects=True, vmem_limit_bytes=60 * 2**20
        ),
        cost_estimate=pl.CostEstimate(
            flops=4 * n * m * queries, bytes_accessed=4 * n * m, transcendentals=0
        ),
    )(query_grads.T, eigenbasis, weights, activations.transpose(1, 0, 2))


def general(query_grads, eigenbasis, eigenvalues, activations):
    grad_block = lax.all_gather(query_grads, "col", axis=0, tiled=True)
    share = eigenbasis.shape[1] // lax.axis_size("row")
    partial_rot = lax.psum_scatter(
        lax.dot_general(
            eigenbasis, grad_block, (((0,), (0,)), ((), ())), preferred_element_type=jnp.float32
        ),
        "row",
        scatter_dimension=0,
        tiled=True,
    )
    local_vals = lax.dynamic_slice_in_dim(eigenvalues, lax.axis_index("row") * share, share, 0)
    filtered = (partial_rot * filter_weights(local_vals)[:, None]).astype(jnp.bfloat16)
    whole_cols = lax.all_gather(filtered, "row", axis=0, tiled=True)
    restored = lax.psum_scatter(
        jnp.dot(eigenbasis, whole_cols, preferred_element_type=jnp.float32),
        "col",
        scatter_dimension=0,
        tiled=True,
    ).astype(jnp.bfloat16)
    blocks = lax.all_gather(restored, "row", axis=0, tiled=True)
    flat = activations.reshape(activations.shape[0], -1)
    return lax.psum_scatter(
        lax.dot_general(blocks, flat, (((0,), (1,)), ((), ())), preferred_element_type=jnp.float32),
        "col",
        scatter_dimension=0,
        tiled=True,
    )


def local(query_grads, eigenbasis, eigenvalues, activations):
    sizes = (lax.axis_size("row"), lax.axis_size("col"))
    fits = (
        sizes == (8, 4)
        and query_grads.shape[1] == 256
        and eigenbasis.shape[1] % (256 * CHUNKS) == 0
        and eigenbasis.shape[0] % 64 == 0
        and activations.shape[0] == 128
    )
    return (fused if fits else general)(query_grads, eigenbasis, eigenvalues, activations)


def solution(mesh):
    in_specs = (P(("row", "col"), None), P("row", "col"), P("col"), P("row", None, "col"))
    out_specs = P("col", "row")
    return jax.shard_map(local, mesh=mesh, in_specs=in_specs, out_specs=out_specs, check_vma=False)
```
